32 devices in a mesh: blk: 8 (over z, y), uly: 4 (over x, core).
Axes of the slice: x: 2, y: 2, z: 4, core: 2. Of those that a mesh axis runs over, the one named last changes fastest.
Arguments:
- queries: bfloat16 [4, 1024, 10240], P('uly', 'blk'), may hold values from -6 to 6
- key_states: bfloat16 [4, 1024, 1024], P('uly', 'blk'), may hold values from -6 to 6
- value_states: bfloat16 [4, 1024, 1024], P('uly', 'blk'), may hold values from -6 to 6
- attention_out: bfloat16 [4, 1024, 10240], P('uly', 'blk'), may hold values from -1.5 to 1.5
- output_grad: bfloat16 [4, 1024, 10240], P('uly', 'blk'), may hold values from -24 to 24
- log_totals: float32 [4, 80, 1024], P('uly', None, 'blk'), as said below
- block_order: int32 [8], replicated, may hold values from 0 to 7, as said below
- query_gain: float32 [128], replicated, may hold values from 0.5 to 1.5
- key_gain: float32 [128], replicated, may hold values from 0.5 to 1.5
Outputs:
- query_grad: bfloat16 [4, 1024, 10240], P('uly', 'blk')
- key_grad: bfloat16 [4, 1024, 1024], P('uly', 'blk')
- value_grad: bfloat16 [4, 1024, 1024], P('uly', 'blk')
- query_gain_grad: float32 [128], replicated
- key_gain_grad: float32 [128], replicated
The draws below stay inside these ranges and needn't reach their ends.
Inputs may be any that keep to these rules, and one draw needn't show every extreme that they name: `block_order`: a permutation; entry b is the place in each sequence of the 128 rows that index b of blk holds. `log_totals`: logarithms of positive softmax totals.
All inputs are finite; a program needn't handle non-finite values.
Results may differ from the reference program's by a relative error of at most 0.0017.
The reference program's roundings to bfloat16 on the way count: a program that leaves them out, or rounds other values in their place, can miss the bound.
Values may be sent and summed in bfloat16 or wider, within the bound.
A program may use at most 320 MiB of HBM per device.

```python
import jax
import jax.numpy as jnp
from jax import lax

HEADS = 80
KV_HEADS = 8
HEAD_DIM = 128
TOK_DEV = 128
GROUP = 10
LENGTH = 1024
SEQS = 4
N_BLK = 8


def sequence_order(key):
    return jax.random.permutation(jax.random.fold_in(key, 101), N_BLK).astype(jnp.int32)


def draw_block_order(key, part):
    order = sequence_order(key)
    return order


def draw_log_totals(key, part):
    order = sequence_order(key)
    key = jax.random.fold_in(key, 5)
    columns = jnp.arange(LENGTH, dtype=jnp.int32)
    places = order[columns // TOK_DEV] * TOK_DEV + columns % TOK_DEV
    offset = jax.random.uniform(key, (SEQS, HEADS, LENGTH), dtype=jnp.float32, minval=0.3, maxval=0.9)
    return jnp.log(places.astype(jnp.float32) + 1.0)[None, None, :] + offset


def steps_of(stream_key, shape, shards, least, high):
    def one(dim, blocks):
        steps = jax.random.uniform(jax.random.fold_in(jax.random.fold_in(stream_key, 6), dim), (blocks,), jnp.float32, least / len(shards), high / len(shards))
        return jnp.repeat(jnp.exp(steps), shape[dim] // blocks).reshape((-1,) + (1,) * (len(shape) - dim - 1))

    level = one(*shards[0])
    for cut in shards[1:]:
        level = level * one(*cut)
    return level


def scatter_about(rng, extent, deviation, bound, cuts=(), kind=jnp.bfloat16):
    loudness = steps_of(rng, extent, cuts, -0.22, 0.18) if cuts else 1.0
    array = jax.random.normal(rng, extent, jnp.float32) * deviation * loudness
    return jnp.minimum(jnp.maximum(array, -bound), bound).astype(kind)


def setup_inputs(seed: int = 0) -> dict:
    key_list = jax.random.split(jax.random.key(seed), 10)
    queries = scatter_about(key_list[0], (SEQS, LENGTH, HEADS * HEAD_DIM), 1.0, 6.0, ((0, 4), (1, 8)))
    key_states = scatter_about(key_list[1], (SEQS, LENGTH, KV_HEADS * HEAD_DIM), 1.0, 6.0, ((0, 4), (1, 8)))
    value_states = scatter_about(key_list[2], (SEQS, LENGTH, KV_HEADS * HEAD_DIM), 1.0, 6.0, ((0, 4), (1, 8)))
    attention_out = scatter_about(key_list[3], (SEQS, LENGTH, HEADS * HEAD_DIM), 0.25, 1.5, ((0, 4), (1, 8)))
    output_grad = scatter_about(key_list[4], (SEQS, LENGTH, HEADS * HEAD_DIM), 4.0, 24.0, ((0, 4), (1, 8)))
    log_totals = draw_log_totals(jax.random.fold_in(key_list[9], 71), 0)
    block_order = draw_block_order(jax.random.fold_in(key_list[9], 71), 0)
    query_gain = jnp.clip(1.0 + 0.1 * jax.random.normal(key_list[7], (HEAD_DIM,), jnp.float32), 0.5, 1.5)
    key_gain = jnp.clip(1.0 + 0.1 * jax.random.normal(key_list[8], (HEAD_DIM,), jnp.float32), 0.5, 1.5)
    return {"queries": queries, "key_states": key_states, "value_states": value_states, "attention_out": attention_out, "output_grad": output_grad, "log_totals": log_totals, "block_order": block_order, "query_gain": query_gain, "key_gain": key_gain}


norm_eps = 1e-06

def normed(states, heads, gain):
    values = states.astype(jnp.float32).reshape(LENGTH, heads, HEAD_DIM)
    inverse = lax.rsqrt(lax.optimization_barrier(jnp.mean(values * values, axis=2, keepdims=True)) + norm_eps)
    unit = values * inverse
    return (unit, inverse, (unit * gain).astype(jnp.bfloat16))

def norm_back(grad, unit, inverse, gain):
    scaled = grad * gain
    inner = lax.optimization_barrier(jnp.mean(scaled * unit, axis=2, keepdims=True))
    return (inverse * (scaled - unit * inner)).astype(jnp.bfloat16)

def reference(queries, key_states, value_states, attention_out, output_grad, log_totals, block_order, query_gain, key_gain):
    rows = jnp.arange(LENGTH, dtype=jnp.int32)
    places = block_order[rows // TOK_DEV] * TOK_DEV + rows % TOK_DEV
    visible = places[None, :] <= places[:, None]
    score_scale = HEAD_DIM ** (-0.5)

    def one_sequence(seq_index):
        query_seq = lax.dynamic_index_in_dim(queries, seq_index, 0, keepdims=False)
        key_seq = lax.dynamic_index_in_dim(key_states, seq_index, 0, keepdims=False)
        value_seq = lax.dynamic_index_in_dim(value_states, seq_index, 0, keepdims=False)
        out_seq = lax.dynamic_index_in_dim(attention_out, seq_index, 0, keepdims=False)
        grad_seq = lax.dynamic_index_in_dim(output_grad, seq_index, 0, keepdims=False)
        totals_seq = lax.dynamic_index_in_dim(log_totals, seq_index, 0, keepdims=False)
        query_unit, query_inverse, query_low = normed(query_seq, HEADS, query_gain)
        key_unit, key_inverse, key_low = normed(key_seq, KV_HEADS, key_gain)
        value_heads = value_seq.reshape(LENGTH, KV_HEADS, HEAD_DIM)
        grad_heads = grad_seq.reshape(LENGTH, HEADS, HEAD_DIM)
        out_heads = out_seq.reshape(LENGTH, HEADS, HEAD_DIM)
        row_inner = lax.optimization_barrier(jnp.sum(grad_heads.astype(jnp.float32) * out_heads.astype(jnp.float32), axis=2))

        def one_head(head_index):
            group_index = head_index // GROUP
            query_one = lax.dynamic_index_in_dim(query_low, head_index, 1, keepdims=False)
            grad_one = lax.dynamic_index_in_dim(grad_heads, head_index, 1, keepdims=False)
            key_one = lax.dynamic_index_in_dim(key_low, group_index, 1, keepdims=False)
            value_one = lax.dynamic_index_in_dim(value_heads, group_index, 1, keepdims=False)
            totals = lax.dynamic_index_in_dim(totals_seq, head_index, 0, keepdims=False)
            inner_one = lax.dynamic_index_in_dim(row_inner, head_index, 1, keepdims=False)
            scores = jnp.dot(query_one, key_one.T, preferred_element_type=jnp.float32) * score_scale
            probs = jnp.where(visible, jnp.exp(scores - totals[:, None]), jnp.zeros_like(scores))
            probs_low = probs.astype(jnp.bfloat16)
            dprobs = jnp.dot(grad_one, value_one.T, preferred_element_type=jnp.float32)
            dscores = (probs * (dprobs - inner_one[:, None])).astype(jnp.bfloat16)
            query_part = jnp.dot(dscores, key_one, preferred_element_type=jnp.float32) * score_scale
            key_part = jnp.dot(dscores.T, query_one, preferred_element_type=jnp.float32) * score_scale
            value_part = jnp.dot(probs_low.T, grad_one, preferred_element_type=jnp.float32)
            return (query_part, key_part, value_part)
        query_parts, key_parts, value_parts = lax.map(one_head, jnp.arange(HEADS, dtype=jnp.int32))
        query_normed_grad = query_parts.transpose(1, 0, 2)
        key_normed_grad = key_parts.reshape(KV_HEADS, GROUP, LENGTH, HEAD_DIM).sum(axis=1).transpose(1, 0, 2)
        value_sum = value_parts.reshape(KV_HEADS, GROUP, LENGTH, HEAD_DIM).sum(axis=1).transpose(1, 0, 2)
        query_term = lax.optimization_barrier(jnp.sum(query_normed_grad * query_unit, axis=(0, 1)))
        key_term = lax.optimization_barrier(jnp.sum(key_normed_grad * key_unit, axis=(0, 1)))
        query_grad = norm_back(query_normed_grad, query_unit, query_inverse, query_gain).reshape(LENGTH, HEADS * HEAD_DIM)
        key_grad = norm_back(key_normed_grad, key_unit, key_inverse, key_gain).reshape(LENGTH, KV_HEADS * HEAD_DIM)
        value_grad = value_sum.reshape(LENGTH, KV_HEADS * HEAD_DIM).astype(jnp.bfloat16)
        return (query_grad, key_grad, value_grad, query_term, key_term)
    query_grad, key_grad, value_grad, query_terms, key_terms = lax.map(one_sequence, jnp.arange(SEQS, dtype=jnp.int32))
    return (query_grad, key_grad, value_grad, lax.optimization_barrier(jnp.sum(query_terms, axis=0)), lax.optimization_barrier(jnp.sum(key_terms, axis=0)))
```

```python
import functools

import jax
import jax.numpy as jnp
from jax import lax
from jax.experimental import pallas as pl
from jax.experimental.pallas import tpu as pltpu
from jax.sharding import PartitionSpec as P

HEADS = 80
KV_HEADS = 8
HEAD_DIM = 128
GROUP = 10
SCALE = HEAD_DIM ** (-0.5)
LOG2E = 1.4426950408889634
PAIRS = GROUP // 2

norm_eps = 1e-06
NT = (((1,), (1,)), ((), ()))
NN = (((1,), (0,)), ((), ()))


def dot(a, b, dims):
    return lax.dot_general(a, b, dims, preferred_element_type=jnp.float32)


def norm_back(grad, unit, inverse, gain):
    scaled = grad * gain
    inner = jnp.mean(scaled * unit, axis=-1, keepdims=True)
    return (inverse * (scaled - unit * inner)).astype(jnp.bfloat16)


def unit_of(values):
    inverse = lax.rsqrt(jnp.mean(values * values, axis=-1, keepdims=True) + norm_eps)
    return values * inverse, inverse


def attend_kernel(
    n_blk, rows, chunk,
    q_ref, do_ref, ao_ref, k_ref, v_ref, lt_ref, bias_ref, gain_ref,
    dq_ref, dk_ref, dv_ref, term_ref,
    qs, dos, stats, kt,
):
    group = pl.program_id(0)
    gain = gain_ref[...]
    lane = lax.broadcasted_iota(jnp.int32, (rows, HEAD_DIM), 1)
    inner = jnp.zeros((rows, HEAD_DIM), jnp.float32)
    for h in range(GROUP):
        cols = slice(h * HEAD_DIM, (h + 1) * HEAD_DIM)
        unit, _ = unit_of(q_ref[:, cols].astype(jnp.float32))
        qs[h // 2, pl.ds((h % 2) * rows, rows), :] = (unit * gain).astype(jnp.bfloat16)
        grad = do_ref[:, cols]
        dos[h // 2, pl.ds((h % 2) * rows, rows), :] = grad
        one = jnp.sum(
            grad.astype(jnp.float32) * ao_ref[:, cols].astype(jnp.float32), axis=1, keepdims=True
        )
        inner = jnp.where(lane == h, one, inner)
    inner = inner.T
    for h in range(GROUP):
        half = pl.ds((h % 2) * rows, rows)
        stats[h // 2, 0:1, half] = inner[h : h + 1, :]
        stats[h // 2, 1:2, half] = lt_ref[0, h : h + 1, :] * LOG2E
    for c in range(n_blk * rows // HEAD_DIM):
        part = pl.ds(c * HEAD_DIM, HEAD_DIM)
        kt[:, part] = k_ref[part, :].astype(jnp.float32).T.astype(jnp.bfloat16)
    dk_ref[...] = jnp.zeros_like(dk_ref)
    dv_ref[...] = jnp.zeros_like(dv_ref)

    @pl.when(group == 0)
    def _():
        term_ref[...] = jnp.zeros_like(term_ref)

    for pair in range(PAIRS):
        query = qs[pair]
        grad = dos[pair]
        row_inner = stats[pair, 0:1, :]
        totals = stats[pair, 1:2, :]
        dq_t = jnp.zeros((HEAD_DIM, 2 * rows), jnp.float32)
        for c in range(n_blk * rows // chunk):
            part = pl.ds(c * chunk, chunk)
            bias = bias_ref[part, :]
            scores = dot(k_ref[part, :], query, NT)
            probs = jnp.exp2(
                scores * (SCALE * LOG2E) - totals + jnp.concatenate([bias, bias], axis=1)
            )
            dprobs = dot(v_ref[part, :], grad, NT)
            dscores = (probs * (dprobs - row_inner)).astype(jnp.bfloat16)
            dv_ref[part, :] += dot(probs.astype(jnp.bfloat16), grad, NN)
            dk_ref[part, :] += dot(dscores, query, NN)
            dq_t += dot(kt[:, part], dscores, NN)
        dq = dq_t.T * SCALE
        for h in range(2):
            cols = pl.ds((2 * pair + h) * HEAD_DIM, HEAD_DIM)
            one = dq[h * rows : (h + 1) * rows, :]
            unit, inverse = unit_of(q_ref[:, cols].astype(jnp.float32))
            term_ref[...] += jnp.sum(one * unit, axis=0, keepdims=True)
            dq_ref[:, cols] = norm_back(one, unit, inverse, gain)


def attend(q, do, ao, k, v, lt, bias, gain, n_blk, rows):
    wide = GROUP * HEAD_DIM
    total = n_blk * rows
    chunk = 2 * rows
    side = pl.BlockSpec((rows, wide), lambda g: (0, g))
    keys = pl.BlockSpec((total, HEAD_DIM), lambda g: (0, g))
    return pl.pallas_call(
        functools.partial(attend_kernel, n_blk, rows, chunk),
        grid=(KV_HEADS,),
        in_specs=[
            side, side, side, keys, keys,
            pl.BlockSpec((1, GROUP, rows), lambda g: (g, 0, 0)),
            pl.BlockSpec((total, rows), lambda g: (0, 0)),
            pl.BlockSpec((1, HEAD_DIM), lambda g: (0, 0)),
        ],
        out_specs=[side, keys, keys, pl.BlockSpec((1, HEAD_DIM), lambda g: (0, 0))],
        out_shape=[
            jax.ShapeDtypeStruct((rows, HEADS * HEAD_DIM), jnp.bfloat16),
            jax.ShapeDtypeStruct((total, KV_HEADS * HEAD_DIM), jnp.float32),
            jax.ShapeDtypeStruct((total, KV_HEADS * HEAD_DIM), jnp.float32),
            jax.ShapeDtypeStruct((1, HEAD_DIM), jnp.float32),
        ],
        scratch_shapes=[
            pltpu.VMEM((PAIRS, 2 * rows, HEAD_DIM), jnp.bfloat16),
            pltpu.VMEM((PAIRS, 2 * rows, HEAD_DIM), jnp.bfloat16),
            pltpu.VMEM((PAIRS, 2, 2 * rows), jnp.float32),
            pltpu.VMEM((HEAD_DIM, total), jnp.bfloat16),
        ],
        compiler_params=pltpu.CompilerParams(
            dimension_semantics=("arbitrary",), vmem_limit_bytes=48 * 1024 * 1024
        ),
        cost_estimate=pl.CostEstimate(
            flops=10 * HEADS * rows * total * HEAD_DIM,
            bytes_accessed=8 * rows * HEADS * HEAD_DIM + 12 * total * KV_HEADS * HEAD_DIM,
            transcendentals=HEADS * rows * total,
        ),
    )(q, do, ao, k, v, lt, bias, gain)


def per_device(
    queries,
    key_states,
    value_states,
    attention_out,
    output_grad,
    log_totals,
    block_order,
    query_gain,
    key_gain,
):
    n_blk = lax.axis_size("blk")
    rows = queries.shape[1]
    key_unit, key_inverse = unit_of(
        key_states[0].astype(jnp.float32).reshape(rows, KV_HEADS, HEAD_DIM)
    )
    key_low = (key_unit * key_gain).astype(jnp.bfloat16).reshape(rows, KV_HEADS * HEAD_DIM)
    k_all = lax.all_gather(key_low, "blk", axis=0, tiled=True)
    v_all = lax.all_gather(value_states[0], "blk", axis=0, tiled=True)
    me = lax.axis_index("blk")
    inside = jnp.arange(rows, dtype=jnp.int32)
    places = (block_order[:, None] * rows + inside[None, :]).reshape(-1)
    own = jnp.sum(jnp.where(jnp.arange(n_blk) == me, block_order, 0)) * rows + inside
    bias = jnp.where(places[:, None] <= own[None, :], 0.0, -jnp.inf).astype(jnp.float32)
    dq, dk, dv, term = attend(
        queries[0], output_grad[0], attention_out[0], k_all, v_all,
        log_totals[0].reshape(KV_HEADS, GROUP, rows), bias, query_gain[None, :], n_blk, rows,
    )
    dk = lax.psum_scatter(dk, "blk", scatter_dimension=0, tiled=True)
    dv = lax.psum_scatter(dv, "blk", scatter_dimension=0, tiled=True)
    key_normed_grad = (dk * SCALE).reshape(rows, KV_HEADS, HEAD_DIM)
    key_term = jnp.sum(key_normed_grad * key_unit, axis=(0, 1))
    query_gain_grad, key_gain_grad = lax.psum((term[0], key_term), ("blk", "uly"))
    key_grad = norm_back(key_normed_grad, key_unit, key_inverse, key_gain).reshape(
        1, rows, KV_HEADS * HEAD_DIM
    )
    return (dq[None], key_grad, dv.astype(jnp.bfloat16)[None], query_gain_grad, key_gain_grad)


def solution(mesh):
    return jax.shard_map(
        per_device,
        mesh=mesh,
        in_specs=(
            P("uly", "blk", None),
            P("uly", "blk", None),
            P("uly", "blk", None),
            P("uly", "blk", None),
            P("uly", "blk", None),
            P("uly", None, "blk"),
            P(),
            P(),
            P(),
        ),
        out_specs=(P("uly", "blk", None), P("uly", "blk", None), P("uly", "blk", None), P(), P()),
        check_vma=False,
    )
```

```python
import functools

import jax
import jax.numpy as jnp
from jax import lax
from jax.experimental import pallas as pl
from jax.experimental.pallas import tpu as pltpu
from jax.sharding import PartitionSpec as P

HEADS = 80
KV_HEADS = 8
HEAD_DIM = 128
GROUP = 10
SCALE = HEAD_DIM ** (-0.5)
LOG2E = 1.4426950408889634
PAIRS = GROUP // 2

norm_eps = 1e-06
NT = (((1,), (1,)), ((), ()))
NN = (((1,), (0,)), ((), ()))


def dot(a, b, dims):
    return lax.dot_general(a, b, dims, preferred_element_type=jnp.float32)


def norm_back(grad, unit, inverse, gain):
    scaled = grad * gain
    inner = jnp.mean(scaled * unit, axis=-1, keepdims=True)
    return (inverse * (scaled - unit * inner)).astype(jnp.bfloat16)


def unit_of(values):
    inverse = lax.rsqrt(jnp.mean(values * values, axis=-1, keepdims=True) + norm_eps)
    return values * inverse, inverse


STEPS = 32000.0
CODE_ROWS = 2 * HEAD_DIM + 16
MESH = pl.DeviceIdType.MESH


def code_half(x):
    most = jnp.maximum(jnp.max(jnp.abs(x), axis=0, keepdims=True), 1e-30)
    power = jnp.ceil(jnp.log2(most))
    return jnp.round(x * (STEPS * jnp.exp2(-power))).astype(jnp.int32).astype(jnp.int16), power


def encode(ref, index, keys, values, rows):
    code, key_power = code_half(keys)
    ref[(*index, pl.ds(0, rows), slice(None))] = code
    code, value_power = code_half(values)
    ref[(*index, pl.ds(rows, rows), slice(None))] = code
    row = lax.broadcasted_iota(jnp.int32, (16, HEAD_DIM), 0)
    powers = jnp.where(row == 0, key_power, value_power)
    ref[(*index, pl.ds(2 * rows, 16), slice(None))] = powers.astype(jnp.int32).astype(jnp.int16)


def as_f32(x):
    return x.astype(jnp.int32).astype(jnp.float32)


def decode(ref, index, rows):
    powers = as_f32(ref[(*index, pl.ds(2 * rows, 16), slice(None))])
    scale = jnp.exp2(powers) * (1.0 / STEPS)
    keys = as_f32(ref[(*index, pl.ds(0, rows), slice(None))]) * scale[0:1, :]
    values = as_f32(ref[(*index, pl.ds(rows, rows), slice(None))]) * scale[1:2, :]
    return keys, values


def fused_kernel(
    n_blk, n_uly, rows,
    q_ref, do_ref, ao_ref, key_ref, value_ref, lt_ref, bias_ref, gain_ref, key_gain_ref,
    dq_ref, dk_ref, dv_ref, q_term_ref, k_term_ref,
    qs, dos, stats, kt, kv, acc, y_out, y_in, z_out, z_in, own_sum, terms, blk_terms, uly_terms,
    kv_send, kv_recv, y_send, y_recv, z_send, z_recv, t_send, t_recv, u_send, u_recv,
):
    n_a = n_blk // 2
    step = pl.program_id(0)
    last = KV_HEADS - 1
    me = lax.axis_index("blk")
    uly = lax.axis_index("uly")
    a = me // 2
    b = me % 2
    partner = me + 1 - 2 * b
    gain = gain_ref[...]
    key_gain = key_gain_ref[...]

    def ring(d):
        return lax.rem(a + d, n_a)

    def kv_copy(g, block, slot, to):
        return pltpu.make_async_remote_copy(
            src_ref=kv.at[g, block], dst_ref=kv.at[g, block],
            send_sem=kv_send.at[g, slot], recv_sem=kv_recv.at[g, block],
            device_id=(to, uly), device_id_type=MESH,
        )

    def send_own(g):
        kv_copy(g, me, n_a - 1, partner).start()
        for d in range(1, n_a):
            kv_copy(g, me, d - 1, ring(d) * 2 + b).start()

    def forward(g):
        for d in range(1, n_a):
            block = ring(d) * 2 + b
            kv_copy(g, block, n_a - 1 + d, partner).wait_recv()
            kv_copy(g, block, n_a - 1 + d, partner).start()

    def gathered(g):
        for d in range(n_a):
            kv_copy(g, ring(d) * 2 + 1 - b, 0, partner).wait_recv()

    def y_copy(g):
        return pltpu.make_async_remote_copy(
            src_ref=y_out.at[g], dst_ref=y_in.at[g],
            send_sem=y_send.at[g], recv_sem=y_recv.at[g],
            device_id=(partner, uly), device_id_type=MESH,
        )

    def z_copy(g, d):
        return pltpu.make_async_remote_copy(
            src_ref=z_out.at[g, d - 1], dst_ref=z_in.at[g, d - 1],
            send_sem=z_send.at[g, d - 1], recv_sem=z_recv.at[g, d - 1],
            device_id=(ring(d) * 2 + b, uly), device_id_type=MESH,
        )

    def send_y(g):
        slot = lax.rem(g, 2)
        for i in range(n_a):
            part = acc.at[slot, i * 2 + 1 - b]
            encode(y_out, (g, i), part[0:rows, :], part[rows : 2 * rows, :], rows)
        y_copy(g).start()

    def send_z(g):
        slot = lax.rem(g, 2)
        y_copy(g).wait_recv()
        for d in range(n_a):
            i = ring(d)
            keys, values = decode(y_in, (g, i), rows)
            part = acc.at[slot, i * 2 + b]
            keys += part[0:rows, :]
            values += part[rows : 2 * rows, :]
            if d == 0:
                own_sum[g, 0:rows, :] = keys
                own_sum[g, rows : 2 * rows, :] = values
            else:
                encode(z_out, (g, d - 1), keys, values, rows)
                z_copy(g, d).start()

    def finish(g):
        keys = own_sum[g, 0:rows, :]
        values = own_sum[g, rows : 2 * rows, :]
        for d in range(1, n_a):
            z_copy(g, d).wait_recv()
            more_keys, more_values = decode(z_in, (g, d - 1), rows)
            keys += more_keys
            values += more_values
        cols = pl.ds(pl.multiple_of(g * HEAD_DIM, HEAD_DIM), HEAD_DIM)
        keys = keys * SCALE
        unit, inverse = unit_of(key_ref[:, cols].astype(jnp.float32))
        terms[1:2, :] += jnp.sum(keys * unit, axis=0, keepdims=True)
        dk_ref[:, cols] = norm_back(keys, unit, inverse, key_gain)
        dv_ref[:, cols] = values.astype(jnp.bfloat16)

    @pl.when(step == 0)
    def _():
        barrier = pltpu.get_barrier_semaphore()
        for d in range(1, n_blk):
            pl.semaphore_signal(
                barrier, inc=1, device_id=(lax.rem(me + d, n_blk), uly), device_id_type=MESH
            )
        for d in range(1, n_uly):
            pl.semaphore_signal(
                barrier, inc=1, device_id=(me, lax.rem(uly + d, n_uly)), device_id_type=MESH
            )
        terms[...] = jnp.zeros_like(terms)
        for g in range(KV_HEADS):
            cols = slice(g * HEAD_DIM, (g + 1) * HEAD_DIM)
            unit, _ = unit_of(key_ref[:, cols].astype(jnp.float32))
            kv[g, me, 0:rows, :] = (unit * key_gain).astype(jnp.bfloat16)
            kv[g, me, rows : 2 * rows, :] = value_ref[:, cols]
        pl.semaphore_wait(barrier, n_blk + n_uly - 2)
        for g in range(AHEAD):
            send_own(g)
        for g in range(AHEAD - 1):
            forward(g)

    @pl.when(step + AHEAD <= last)
    def _():
        send_own(step + AHEAD)

    @pl.when(step + AHEAD - 1 <= last)
    def _():
        forward(step + AHEAD - 1)

    @pl.when(step >= 2)
    def _():
        finish(step - 2)

    lane = lax.broadcasted_iota(jnp.int32, (rows, HEAD_DIM), 1)
    inner = jnp.zeros((rows, HEAD_DIM), jnp.float32)
    for h in range(GROUP):
        cols = slice(h * HEAD_DIM, (h + 1) * HEAD_DIM)
        unit, _ = unit_of(q_ref[:, cols].astype(jnp.float32))
        qs[h // 2, pl.ds((h % 2) * rows, rows), :] = (unit * gain).astype(jnp.bfloat16)
        grad = do_ref[:, cols]
        dos[h // 2, pl.ds((h % 2) * rows, rows), :] = grad
        one = jnp.sum(
            grad.astype(jnp.float32) * ao_ref[:, cols].astype(jnp.float32), axis=1, keepdims=True
        )
        inner = jnp.where(lane == h, one, inner)
    inner = inner.T
    for h in range(GROUP):
        half = pl.ds((h % 2) * rows, rows)
        stats[h // 2, 0:1, half] = inner[h : h + 1, :]
        stats[h // 2, 1:2, half] = lt_ref[0, h : h + 1, :] * LOG2E

    gathered(step)
    slot = lax.rem(step, 2)
    for i in range(n_blk):
        kt[:, i * rows : (i + 1) * rows] = (
            kv[step, i, 0:rows, :].astype(jnp.float32).T.astype(jnp.bfloat16)
        )
    acc[slot] = jnp.zeros((n_blk, 2 * rows, HEAD_DIM), jnp.float32)

    def one_pair(pair, carry):
        query = qs[pair]
        grad = dos[pair]
        row_inner = stats[pair, 0:1, :]
        totals = stats[pair, 1:2, :]
        dq_t = jnp.zeros((HEAD_DIM, 2 * rows), jnp.float32)
        for c in range(n_a):
            both = pl.ds(2 * c, 2)
            part = pl.ds(c * 2 * rows, 2 * rows)
            keys = kv[step, both, 0:rows, :].reshape(2 * rows, HEAD_DIM)
            values = kv[step, both, rows : 2 * rows, :].reshape(2 * rows, HEAD_DIM)
            bias = bias_ref[part, :]
            scores = dot(keys, query, NT)
            probs = jnp.exp2(
                scores * (SCALE * LOG2E) - totals + jnp.concatenate([bias, bias], axis=1)
            )
            dprobs = dot(values, grad, NT)
            dscores = (probs * (dprobs - row_inner)).astype(jnp.bfloat16)
            acc[slot, both, rows : 2 * rows, :] += dot(
                probs.astype(jnp.bfloat16), grad, NN
            ).reshape(2, rows, HEAD_DIM)
            acc[slot, both, 0:rows, :] += dot(dscores, query, NN).reshape(2, rows, HEAD_DIM)
            dq_t += dot(kt[:, part], dscores, NN)
        dq = dq_t.T * SCALE
        for h in range(2):
            cols = pl.ds(pl.multiple_of((2 * pair + h) * HEAD_DIM, HEAD_DIM), HEAD_DIM)
            one = dq[h * rows : (h + 1) * rows, :]
            unit, inverse = unit_of(q_ref[:, cols].astype(jnp.float32))
            terms[0:1, :] += jnp.sum(one * unit, axis=0, keepdims=True)
            dq_ref[:, cols] = norm_back(one, unit, inverse, gain)
        return carry

    lax.fori_loop(0, PAIRS, one_pair, 0)
    send_y(step)

    @pl.when(step >= 1)
    def _():
        send_z(step - 1)

    @pl.when(step == last)
    def _():
        finish(last - 1)
        send_z(last)
        finish(last)

        def term_copy(ref, index, sends, recvs, d, to):
            return pltpu.make_async_remote_copy(
                src_ref=ref.at[index], dst_ref=ref.at[index],
                send_sem=sends.at[d - 1], recv_sem=recvs.at[index],
                device_id=to, device_id_type=MESH,
            )

        def share(ref, mine, count, sends, recvs, to):
            for d in range(1, count):
                term_copy(ref, mine, sends, recvs, d, to(d)).start()
            for d in range(1, count):
                term_copy(ref, lax.rem(mine + d, count), sends, recvs, d, to(d)).wait_recv()
            total = ref[0]
            for i in range(1, count):
                total = total + ref[i]
            return total

        blk_terms[me] = terms[...]
        uly_terms[uly] = share(
            blk_terms, me, n_blk, t_send, t_recv, lambda d: (lax.rem(me + d, n_blk), uly)
        )
        total = share(
            uly_terms, uly, n_uly, u_send, u_recv, lambda d: (me, lax.rem(uly + d, n_uly))
        )
        q_term_ref[...] = total[0:1, :]
        k_term_ref[...] = total[1:2, :]
        for d in range(1, n_blk):
            term_copy(blk_terms, me, t_send, t_recv, d, (lax.rem(me + d, n_blk), uly)).wait_send()
        for d in range(1, n_uly):
            term_copy(uly_terms, uly, u_send, u_recv, d, (me, lax.rem(uly + d, n_uly))).wait_send()

        def drain(g, carry):
            for slot in range(2 * n_a - 1):
                kv_copy(g, me, slot, partner).wait_send()
            y_copy(g).wait_send()
            for d in range(1, n_a):
                z_copy(g, d).wait_send()
            return carry

        lax.fori_loop(0, KV_HEADS, drain, 0)


AHEAD = 3


def fused(q, do, ao, keys, values, lt, bias, gain, key_gain, n_blk, n_uly, rows):
    wide = GROUP * HEAD_DIM
    total = n_blk * rows
    n_a = n_blk // 2
    dma = pltpu.SemaphoreType.DMA
    side = pl.BlockSpec((rows, wide), lambda g: (0, g))
    whole = pl.BlockSpec((rows, KV_HEADS * HEAD_DIM), lambda g: (0, 0))
    line = pl.BlockSpec((1, HEAD_DIM), lambda g: (0, 0))
    code = (CODE_ROWS, HEAD_DIM)
    return pl.pallas_call(
        functools.partial(fused_kernel, n_blk, n_uly, rows),
        grid=(KV_HEADS,),
        in_specs=[
            side, side, side, whole, whole,
            pl.BlockSpec((1, GROUP, rows), lambda g: (g, 0, 0)),
            pl.BlockSpec((total, rows), lambda g: (0, 0)),
            line, line,
        ],
        out_specs=[side, whole, whole, line, line],
        out_shape=[
            jax.ShapeDtypeStruct((rows, HEADS * HEAD_DIM), jnp.bfloat16),
            jax.ShapeDtypeStruct((rows, KV_HEADS * HEAD_DIM), jnp.bfloat16),
            jax.ShapeDtypeStruct((rows, KV_HEADS * HEAD_DIM), jnp.bfloat16),
            jax.ShapeDtypeStruct((1, HEAD_DIM), jnp.float32),
            jax.ShapeDtypeStruct((1, HEAD_DIM), jnp.float32),
        ],
        scratch_shapes=[
            pltpu.VMEM((PAIRS, 2 * rows, HEAD_DIM), jnp.bfloat16),
            pltpu.VMEM((PAIRS, 2 * rows, HEAD_DIM), jnp.bfloat16),
            pltpu.VMEM((PAIRS, 2, 2 * rows), jnp.float32),
            pltpu.VMEM((HEAD_DIM, total), jnp.bfloat16),
            pltpu.VMEM((KV_HEADS, n_blk, 2 * rows, HEAD_DIM), jnp.bfloat16),
            pltpu.VMEM((2, n_blk, 2 * rows, HEAD_DIM), jnp.float32),
            pltpu.VMEM((KV_HEADS, n_a, *code), jnp.int16),
            pltpu.VMEM((KV_HEADS, n_a, *code), jnp.int16),
            pltpu.VMEM((KV_HEADS, n_a - 1, *code), jnp.int16),
            pltpu.VMEM((KV_HEADS, n_a - 1, *code), jnp.int16),
            pltpu.VMEM((KV_HEADS, 2 * rows, HEAD_DIM), jnp.float32),
            pltpu.VMEM((8, HEAD_DIM), jnp.float32),
            pltpu.VMEM((n_blk, 8, HEAD_DIM), jnp.float32),
            pltpu.VMEM((n_uly, 8, HEAD_DIM), jnp.float32),
            dma((KV_HEADS, 2 * n_a - 1)),
            dma((KV_HEADS, n_blk)),
            dma((KV_HEADS,)),
            dma((KV_HEADS,)),
            dma((KV_HEADS, n_a - 1)),
            dma((KV_HEADS, n_a - 1)),
            dma((n_blk - 1,)),
            dma((n_blk,)),
            dma((n_uly - 1,)),
            dma((n_uly,)),
        ],
        compiler_params=pltpu.CompilerParams(
            dimension_semantics=("arbitrary",),
            vmem_limit_bytes=56 * 1024 * 1024,
            collective_id=0,
            has_side_effects=True,
        ),
        cost_estimate=pl.CostEstimate(
            flops=10 * HEADS * rows * total * HEAD_DIM,
            bytes_accessed=8 * rows * HEADS * HEAD_DIM,
            transcendentals=HEADS * rows * total,
        ),
    )(q, do, ao, keys, values, lt, bias, gain, key_gain)


def per_device(
    queries,
    key_states,
    value_states,
    attention_out,
    output_grad,
    log_totals,
    block_order,
    query_gain,
    key_gain,
):
    n_blk = lax.axis_size("blk")
    n_uly = lax.axis_size("uly")
    rows = queries.shape[1]
    me = lax.axis_index("blk")
    inside = jnp.arange(rows, dtype=jnp.int32)
    places = (block_order[:, None] * rows + inside[None, :]).reshape(-1)
    own = jnp.sum(jnp.where(jnp.arange(n_blk) == me, block_order, 0)) * rows + inside
    bias = jnp.where(places[:, None] <= own[None, :], 0.0, -jnp.inf).astype(jnp.float32)
    dq, dk, dv, query_term, key_term = fused(
        queries[0], output_grad[0], attention_out[0], key_states[0], value_states[0],
        log_totals[0].reshape(KV_HEADS, GROUP, rows), bias, query_gain[None, :],
        key_gain[None, :], n_blk, n_uly, rows,
    )
    return (dq[None], dk[None], dv[None], query_term[0], key_term[0])


def solution(mesh):
    return jax.shard_map(
        per_device,
        mesh=mesh,
        in_specs=(
            P("uly", "blk", None),
            P("uly", "blk", None),
            P("uly", "blk", None),
            P("uly", "blk", None),
            P("uly", "blk", None),
            P("uly", None, "blk"),
            P(),
            P(),
            P(),
        ),
        out_specs=(P("uly", "blk", None), P("uly", "blk", None), P("uly", "blk", None), P(), P()),
        check_vma=False,
    )
```

```python
import functools

import jax
import jax.numpy as jnp
from jax import lax
from jax.experimental import pallas as pl
from jax.experimental.pallas import tpu as pltpu
from jax.sharding import PartitionSpec as P

HEADS = 80
KV_HEADS = 8
HEAD_DIM = 128
GROUP = 10
SCALE = HEAD_DIM ** (-0.5)
LOG2E = 1.4426950408889634
PAIRS = GROUP // 2

norm_eps = 1e-06
NT = (((1,), (1,)), ((), ()))
NN = (((1,), (0,)), ((), ()))


def dot(a, b, dims):
    return lax.dot_general(a, b, dims, preferred_element_type=jnp.float32)


def norm_back(grad, unit, inverse, gain):
    scaled = grad * gain
    inner = jnp.mean(scaled * unit, axis=-1, keepdims=True)
    return (inverse * (scaled - unit * inner)).astype(jnp.bfloat16)


def unit_of(values):
    inverse = lax.rsqrt(jnp.mean(values * values, axis=-1, keepdims=True) + norm_eps)
    return values * inverse, inverse


STEPS = 32000.0
CODE_ROWS = HEAD_DIM + 16
MESH = pl.DeviceIdType.MESH


def encode(ref, index, x, rows):
    most = jnp.maximum(jnp.max(jnp.abs(x), axis=0, keepdims=True), 1e-30)
    power = jnp.ceil(jnp.log2(most))
    code = jnp.round(x * (STEPS * jnp.exp2(-power))).astype(jnp.int32).astype(jnp.int16)
    ref[(*index, pl.ds(0, rows), slice(None))] = code
    powers = jnp.broadcast_to(power, (16, HEAD_DIM))
    ref[(*index, pl.ds(rows, 16), slice(None))] = powers.astype(jnp.int32).astype(jnp.int16)


def as_f32(x):
    return x.astype(jnp.int32).astype(jnp.float32)


def decode(ref, index, rows):
    powers = as_f32(ref[(*index, pl.ds(rows, 16), slice(None))])
    scale = jnp.exp2(powers[0:1, :]) * (1.0 / STEPS)
    return as_f32(ref[(*index, pl.ds(0, rows), slice(None))]) * scale


def fused_kernel(
    n_blk, n_uly, rows,
    q_ref, do_ref, ao_ref, key_ref, value_ref, lt_ref, bias_ref, gain_ref, key_gain_ref,
    dq_ref, dk_ref, dv_ref, q_term_ref, k_term_ref,
    qs, dos, stats, kt, kv, acc, y_out, y_in, line_out, line_in, v_out, v_in,
    terms, blk_terms, uly_terms,
    kv_send, kv_recv, y_send, y_recv, line_send, line_recv, v_send, v_recv,
    t_send, t_recv, u_send, u_recv,
):
    n_a = n_blk // 2
    now = pl.program_id(0)
    step = now - n_a
    last = KV_HEADS - 1
    me = lax.axis_index("blk")
    uly = lax.axis_index("uly")
    a = me // 2
    b = me % 2
    other = 1 - b
    partner = a * 2 + other
    gain = gain_ref[...]
    key_gain = key_gain_ref[...]
    LEFT, RIGHT, ACROSS = 0, 1, 2

    def reach(way):
        return (me - 2, me + 2, partner)[way]

    def has(way):
        return a > 0 if way == LEFT else a < n_a - 1

    def kv_copy(which, g, block, way):
        return pltpu.make_async_remote_copy(
            src_ref=kv.at[which, g, block], dst_ref=kv.at[which, g, block],
            send_sem=kv_send.at[which, g, block, way], recv_sem=kv_recv.at[which, g, block],
            device_id=(reach(way), uly), device_id_type=MESH,
        )

    def send_on(which, g, block, way):
        @pl.when(has(way))
        def _():
            kv_copy(which, g, block, way).start()

    def gather_stage(s, g):
        if s == 0:
            for which in range(2):
                kv_copy(which, g, me, ACROSS).start()
                send_on(which, g, me, LEFT)
                send_on(which, g, me, RIGHT)
            return
        if s == 1:
            kv_copy(1, g, partner, ACROSS).wait_recv()
            send_on(1, g, partner, LEFT)
            send_on(1, g, partner, RIGHT)
        for way, shift in ((RIGHT, -1), (LEFT, 1)):
            far = a + shift * s
            near = a + shift * (s - 1)

            @pl.when((far >= 0) & (far < n_a))
            def _():
                for which in range(2):
                    kv_copy(which, g, far * 2 + b, way).wait_recv()
                    if which == 0:
                        kv_copy(which, g, far * 2 + b, ACROSS).start()
                    send_on(which, g, far * 2 + b, way)

            if s > 1:
                @pl.when((near >= 0) & (near < n_a))
                def _():
                    kv_copy(1, g, near * 2 + other, way).wait_recv()
                    if s < n_a:
                        send_on(1, g, near * 2 + other, way)

    def gathered(g):
        gather_stage(n_a, g)
        for i in range(n_a):
            kv_copy(0, g, i * 2 + other, ACROSS).wait_recv()

    def y_copy(g):
        return pltpu.make_async_remote_copy(
            src_ref=y_out.at[g], dst_ref=y_in.at[g],
            send_sem=y_send.at[g], recv_sem=y_recv.at[g],
            device_id=(partner, uly), device_id_type=MESH,
        )

    def v_copy(g):
        return pltpu.make_async_remote_copy(
            src_ref=v_out.at[g], dst_ref=v_in.at[g],
            send_sem=v_send.at[g], recv_sem=v_recv.at[g],
            device_id=(partner, uly), device_id_type=MESH,
        )

    def line_copy(kind, g, way, d):
        return pltpu.make_async_remote_copy(
            src_ref=line_out.at[kind, g, way, d - 1], dst_ref=line_in.at[kind, g, way, d - 1],
            send_sem=line_send.at[kind, g, way, d - 1], recv_sem=line_recv.at[kind, g, way, d - 1],
            device_id=(reach(way), uly), device_id_type=MESH,
        )

    def part_of(kind, i):
        return (0 if kind == 0 else 1), i * 2 + (other if kind == 2 else b)

    def line_stage(kind, g, d):
        for way, shift in ((RIGHT, 1), (LEFT, -1)):
            to = a + shift * d

            @pl.when((to >= 0) & (to < n_a))
            def _():
                half, block = part_of(kind, to)
                at = pl.ds(half * rows, rows)
                if d < n_a - 1:
                    @pl.when(has(1 - way))
                    def _():
                        line_copy(kind, g, way, d + 1).wait_recv()
                        acc[g, block, at, :] += decode(line_in, (kind, g, way, d), rows)
                encode(line_out, (kind, g, way, d - 1), acc[g, block, at, :], rows)
                line_copy(kind, g, way, d).start()

    def line_end(kind, g):
        half, block = part_of(kind, a)
        at = pl.ds(half * rows, rows)
        for way in (RIGHT, LEFT):
            @pl.when(has(1 - way))
            def _():
                line_copy(kind, g, way, 1).wait_recv()
                acc[g, block, at, :] += decode(line_in, (kind, g, way, 0), rows)
        return acc[g, block, at, :]

    def return_stage(k, g):
        if k == 1:
            for i in range(n_a):
                encode(y_out, (g, i), acc[g, i * 2 + other, 0:rows, :], rows)
            y_copy(g).start()
        if k <= n_a - 1:
            line_stage(2, g, n_a - k)
            line_stage(1, g, n_a - k)
        if k == 2:
            y_copy(g).wait_recv()
            for i in range(n_a):
                acc[g, i * 2 + b, 0:rows, :] += decode(y_in, (g, i), rows)
        if 2 <= k <= n_a:
            line_stage(0, g, n_a - k + 1)
        if k == n_a:
            encode(v_out, (g,), line_end(2, g), rows)
            v_copy(g).start()
            line_end(1, g)
        if k == n_a + 1:
            cols = pl.ds(pl.multiple_of(g * HEAD_DIM, HEAD_DIM), HEAD_DIM)
            keys = line_end(0, g) * SCALE
            unit, inverse = unit_of(key_ref[:, cols].astype(jnp.float32))
            terms[1:2, :] += jnp.sum(keys * unit, axis=0, keepdims=True)
            dk_ref[:, cols] = norm_back(keys, unit, inverse, key_gain)
            v_copy(g).wait_recv()
            values = acc[g, me, rows : 2 * rows, :] + decode(v_in, (g,), rows)
            dv_ref[:, cols] = values.astype(jnp.bfloat16)

    @pl.when(now == 0)
    def _():
        barrier = pltpu.get_barrier_semaphore()
        for d in range(1, n_blk):
            pl.semaphore_signal(
                barrier, inc=1, device_id=(lax.rem(me + d, n_blk), uly), device_id_type=MESH
            )
        for d in range(1, n_uly):
            pl.semaphore_signal(
                barrier, inc=1, device_id=(me, lax.rem(uly + d, n_uly)), device_id_type=MESH
            )
        terms[...] = jnp.zeros_like(terms)
        for g in range(KV_HEADS):
            cols = slice(g * HEAD_DIM, (g + 1) * HEAD_DIM)
            unit, _ = unit_of(key_ref[:, cols].astype(jnp.float32))
            kv[0, g, me] = (unit * key_gain).astype(jnp.bfloat16)
            kv[1, g, me] = value_ref[:, cols]
        pl.semaphore_wait(barrier, n_blk + n_uly - 2)

    def attend():
        lane = lax.broadcasted_iota(jnp.int32, (rows, HEAD_DIM), 1)
        inner = jnp.zeros((rows, HEAD_DIM), jnp.float32)
        for h in range(GROUP):
            cols = slice(h * HEAD_DIM, (h + 1) * HEAD_DIM)
            unit, _ = unit_of(q_ref[:, cols].astype(jnp.float32))
            qs[h // 2, pl.ds((h % 2) * rows, rows), :] = (unit * gain).astype(jnp.bfloat16)
            grad = do_ref[:, cols]
            dos[h // 2, pl.ds((h % 2) * rows, rows), :] = grad
            one = jnp.sum(
                grad.astype(jnp.float32) * ao_ref[:, cols].astype(jnp.float32), axis=1, keepdims=True
            )
            inner = jnp.where(lane == h, one, inner)
        inner = inner.T
        for h in range(GROUP):
            half = pl.ds((h % 2) * rows, rows)
            stats[h // 2, 0:1, half] = inner[h : h + 1, :]
            stats[h // 2, 1:2, half] = lt_ref[0, h : h + 1, :] * LOG2E

        gathered(step)
        slot = step
        for i in range(n_blk):
            kt[:, i * rows : (i + 1) * rows] = (
                kv[0, step, i].astype(jnp.float32).T.astype(jnp.bfloat16)
            )

        def one_pair(pair):
            query = qs[pair]
            grad = dos[pair]
            row_inner = stats[pair, 0:1, :]
            totals = stats[pair, 1:2, :]
            dq_t = jnp.zeros((HEAD_DIM, 2 * rows), jnp.float32)
            for c in range(n_a):
                both = pl.ds(2 * c, 2)
                part = pl.ds(c * 2 * rows, 2 * rows)
                keys = kv[0, step, both].reshape(2 * rows, HEAD_DIM)
                values = kv[1, step, both].reshape(2 * rows, HEAD_DIM)
                bias = bias_ref[part, :]
                scores = dot(keys, query, NT)
                probs = jnp.exp2(
                    scores * (SCALE * LOG2E) - totals + jnp.concatenate([bias, bias], axis=1)
                )
                dprobs = dot(values, grad, NT)
                dscores = (probs * (dprobs - row_inner)).astype(jnp.bfloat16)
                value_part = dot(probs.astype(jnp.bfloat16), grad, NN).reshape(2, rows, HEAD_DIM)
                key_part = dot(dscores, query, NN).reshape(2, rows, HEAD_DIM)
                if pair > 0:
                    value_part += acc[slot, both, rows : 2 * rows, :]
                    key_part += acc[slot, both, 0:rows, :]
                acc[slot, both, rows : 2 * rows, :] = value_part
                acc[slot, both, 0:rows, :] = key_part
                dq_t += dot(kt[:, part], dscores, NN)
            dq = dq_t.T * SCALE
            for h in range(2):
                cols = pl.ds((2 * pair + h) * HEAD_DIM, HEAD_DIM)
                one = dq[h * rows : (h + 1) * rows, :]
                unit, inverse = unit_of(q_ref[:, cols].astype(jnp.float32))
                terms[0:1, :] += jnp.sum(one * unit, axis=0, keepdims=True)
                dq_ref[:, cols] = norm_back(one, unit, inverse, gain)

        for pair in range(PAIRS):
            one_pair(pair)

    for s in range(n_a):
        @pl.when((now - s >= 0) & (now - s <= last))
        def _():
            gather_stage(s, now - s)

    @pl.when((step >= 0) & (step <= last))
    def _():
        attend()

    for k in range(1, n_a + 2):
        @pl.when((step - k + 1 >= 0) & (step - k + 1 <= last))
        def _():
            return_stage(k, step - k + 1)

    @pl.when(step == last + n_a)
    def _():
        def term_copy(ref, index, sends, recvs, d, to):
            return pltpu.make_async_remote_copy(
                src_ref=ref.at[index], dst_ref=ref.at[index],
                send_sem=sends.at[d - 1], recv_sem=recvs.at[index],
                device_id=to, device_id_type=MESH,
            )

        def share(ref, mine, count, sends, recvs, to):
            for d in range(1, count):
                term_copy(ref, mine, sends, recvs, d, to(d)).start()
            for d in range(1, count):
                term_copy(ref, lax.rem(mine + d, count), sends, recvs, d, to(d)).wait_recv()
            total = ref[0]
            for i in range(1, count):
                total = total + ref[i]
            return total

        blk_terms[me] = terms[...]
        uly_terms[uly] = share(
            blk_terms, me, n_blk, t_send, t_recv, lambda d: (lax.rem(me + d, n_blk), uly)
        )
        total = share(
            uly_terms, uly, n_uly, u_send, u_recv, lambda d: (me, lax.rem(uly + d, n_uly))
        )
        q_term_ref[...] = total[0:1, :]
        k_term_ref[...] = total[1:2, :]
        for d in range(1, n_blk):
            term_copy(blk_terms, me, t_send, t_recv, d, (lax.rem(me + d, n_blk), uly)).wait_send()
        for d in range(1, n_uly):
            term_copy(uly_terms, uly, u_send, u_recv, d, (me, lax.rem(uly + d, n_uly))).wait_send()

        def when_started(condition, copy):
            @pl.when(condition)
            def _():
                copy.wait_send()

        def drain(g, carry):
            for which in range(2):
                kv_copy(which, g, me, ACROSS).wait_send()
                for way, shift in ((RIGHT, -1), (LEFT, 1)):
                    when_started(has(way), kv_copy(which, g, me, way))
                    if which == 1:
                        when_started(has(way), kv_copy(1, g, partner, way))
                    for d in range(1, n_a):
                        far = a + shift * d
                        inside = (far >= 0) & (far < n_a)
                        on = inside & has(way)
                        when_started(on, kv_copy(which, g, far * 2 + b, way))
                        if which == 0:
                            when_started(inside, kv_copy(0, g, far * 2 + b, ACROSS))
                        else:
                            when_started(on, kv_copy(1, g, far * 2 + other, way))
            y_copy(g).wait_send()
            v_copy(g).wait_send()
            for kind in range(3):
                for d in range(1, n_a):
                    when_started(a + d < n_a, line_copy(kind, g, RIGHT, d))
                    when_started(a - d >= 0, line_copy(kind, g, LEFT, d))
            return carry

        lax.fori_loop(0, KV_HEADS, drain, 0)


def fused(q, do, ao, keys, values, lt, bias, gain, key_gain, n_blk, n_uly, rows):
    wide = GROUP * HEAD_DIM
    total = n_blk * rows
    n_a = n_blk // 2
    dma = pltpu.SemaphoreType.DMA
    head = lambda i: jnp.clip(i - n_a, 0, KV_HEADS - 1)
    side = pl.BlockSpec((rows, wide), lambda i: (0, head(i)))
    whole = pl.BlockSpec((rows, KV_HEADS * HEAD_DIM), lambda g: (0, 0))
    line = pl.BlockSpec((1, HEAD_DIM), lambda g: (0, 0))
    code = (CODE_ROWS, HEAD_DIM)
    return pl.pallas_call(
        functools.partial(fused_kernel, n_blk, n_uly, rows),
        grid=(KV_HEADS + 2 * n_a,),
        in_specs=[
            side, side, side, whole, whole,
            pl.BlockSpec((1, GROUP, rows), lambda i: (head(i), 0, 0)),
            pl.BlockSpec((total, rows), lambda g: (0, 0)),
            line, line,
        ],
        out_specs=[side, whole, whole, line, line],
        out_shape=[
            jax.ShapeDtypeStruct((rows, HEADS * HEAD_DIM), jnp.bfloat16),
            jax.ShapeDtypeStruct((rows, KV_HEADS * HEAD_DIM), jnp.bfloat16),
            jax.ShapeDtypeStruct((rows, KV_HEADS * HEAD_DIM), jnp.bfloat16),
            jax.ShapeDtypeStruct((1, HEAD_DIM), jnp.float32),
            jax.ShapeDtypeStruct((1, HEAD_DIM), jnp.float32),
        ],
        scratch_shapes=[
            pltpu.VMEM((PAIRS, 2 * rows, HEAD_DIM), jnp.bfloat16),
            pltpu.VMEM((PAIRS, 2 * rows, HEAD_DIM), jnp.bfloat16),
            pltpu.VMEM((PAIRS, 2, 2 * rows), jnp.float32),
            pltpu.VMEM((HEAD_DIM, total), jnp.bfloat16),
            pltpu.VMEM((2, KV_HEADS, n_blk, rows, HEAD_DIM), jnp.bfloat16),
            pltpu.VMEM((KV_HEADS, n_blk, 2 * rows, HEAD_DIM), jnp.float32),
            pltpu.VMEM((KV_HEADS, n_a, *code), jnp.int16),
            pltpu.VMEM((KV_HEADS, n_a, *code), jnp.int16),
            pltpu.VMEM((3, KV_HEADS, 2, n_a - 1, *code), jnp.int16),
            pltpu.VMEM((3, KV_HEADS, 2, n_a - 1, *code), jnp.int16),
            pltpu.VMEM((KV_HEADS, *code), jnp.int16),
            pltpu.VMEM((KV_HEADS, *code), jnp.int16),
            pltpu.VMEM((8, HEAD_DIM), jnp.float32),
            pltpu.VMEM((n_blk, 8, HEAD_DIM), jnp.float32),
            pltpu.VMEM((n_uly, 8, HEAD_DIM), jnp.float32),
            dma((2, KV_HEADS, n_blk, 3)),
            dma((2, KV_HEADS, n_blk)),
            dma((KV_HEADS,)),
            dma((KV_HEADS,)),
            dma((3, KV_HEADS, 2, n_a - 1)),
            dma((3, KV_HEADS, 2, n_a - 1)),
            dma((KV_HEADS,)),
            dma((KV_HEADS,)),
            dma((n_blk - 1,)),
            dma((n_blk,)),
            dma((n_uly - 1,)),
            dma((n_uly,)),
        ],
        compiler_params=pltpu.CompilerParams(
            dimension_semantics=("arbitrary",),
            vmem_limit_bytes=60 * 1024 * 1024,
            collective_id=0,
            has_side_effects=True,
        ),
        cost_estimate=pl.CostEstimate(
            flops=10 * HEADS * rows * total * HEAD_DIM,
            bytes_accessed=8 * rows * HEADS * HEAD_DIM,
            transcendentals=HEADS * rows * total,
        ),
    )(q, do, ao, keys, values, lt, bias, gain, key_gain)


def per_device(
    queries,
    key_states,
    value_states,
    attention_out,
    output_grad,
    log_totals,
    block_order,
    query_gain,
    key_gain,
):
    n_blk = lax.axis_size("blk")
    n_uly = lax.axis_size("uly")
    rows = queries.shape[1]
    me = lax.axis_index("blk")
    inside = jnp.arange(rows, dtype=jnp.int32)
    places = (block_order[:, None] * rows + inside[None, :]).reshape(-1)
    own = jnp.sum(jnp.where(jnp.arange(n_blk) == me, block_order, 0)) * rows + inside
    bias = jnp.where(places[:, None] <= own[None, :], 0.0, -jnp.inf).astype(jnp.float32)
    dq, dk, dv, query_term, key_term = fused(
        queries[0], output_grad[0], attention_out[0], key_states[0], value_states[0],
        log_totals[0].reshape(KV_HEADS, GROUP, rows), bias, query_gain[None, :],
        key_gain[None, :], n_blk, n_uly, rows,
    )
    return (dq[None], dk[None], dv[None], query_term[0], key_term[0])


def solution(mesh):
    return jax.shard_map(
        per_device,
        mesh=mesh,
        in_specs=(
            P("uly", "blk", None),
            P("uly", "blk", None),
            P("uly", "blk", None),
            P("uly", "blk", None),
            P("uly", "blk", None),
            P("uly", None, "blk"),
            P(),
            P(),
            P(),
        ),
        out_specs=(P("uly", "blk", None), P("uly", "blk", None), P("uly", "blk", None), P(), P()),
        check_vma=False,
    )
```
